512 devices in a mesh: gene: 16 (over y, z_lo), prot: 32 (over x, z_hi, core).
Axes of the slice: x: 4, y: 8, z: 8 (z_hi: 4, z_lo: 2; z = z_hi * 2 + z_lo), core: 2. Of those that a mesh axis runs over, the one named last changes fastest.
Arguments:
- density: float32 [256, 192, 16, 128], P('gene', 'prot'), may hold values from 0 to 2
- levels: float32 [8], replicated, may hold values from 0.1 to 0.9
- rate_index: int32 [256, 3], P('gene'), may hold values from 0 to 7
- on_rate: float32 [8], replicated, may hold values from 0.2 to 3
- off_rate: float32 [8], replicated, may hold values from 0.2 to 3
- gene_order: int32 [4], replicated, may hold values from 0 to 3, each once
Outputs:
- evolved: float32 [256, 192, 16, 128], P('gene', 'prot')
The draws below stay inside these ranges and needn't reach their ends.
Inputs may be any that keep to these rules, and one draw needn't show every extreme that they name: `gene_order`: a permutation of 0 to 3.
All inputs are finite; a program needn't handle non-finite values.
Results may differ from the reference program's by a relative error of at most 0.00002.
Values sent between devices are 32-bit elements; how exact they have to be, the bound alone decides.
No kernel may reach another device: no remote copies, remote signals or barrier semaphores. Data moves between devices by JAX's collectives and lax.ppermute only.
A program may use at most 64 MiB of HBM per device.

```python
import math
import jax
import jax.numpy as jnp
from jax import lax

STATE_BITS = 8
LEVELS = 8
BLOCKS = 4
SUBSTEPS = 6
NY = 16
NZ = 128
STATES = 256
NX = 192


def touch_ends(values, stream_key, least, top_value):
    spot = [jax.random.randint(jax.random.fold_in(stream_key, axis), (), 0, length) for axis, length in enumerate(values.shape)]
    widest = values.shape.index(max(values.shape))
    neighbour = spot[:widest] + [(spot[widest] + 1) % values.shape[widest]] + spot[widest + 1:]
    return values.at[tuple(spot)].set(least).at[tuple(neighbour)].set(top_value)


def shard_levels(stream_key, shape, split, least, top_value):
    loudness, own = 1.0, jax.random.fold_in(stream_key, 6)
    for axis_at, parts in split:
        heights = jnp.exp(jax.random.uniform(jax.random.fold_in(own, axis_at), (parts,), jnp.float32, least / len(split), top_value / len(split)))
        loudness = loudness * jnp.repeat(heights, shape[axis_at] // parts).reshape([-1 if axis == axis_at else 1 for axis in range(len(shape))])
    return loudness


def setup_inputs(seed: int = 0) -> dict:
    splits = jax.random.split(jax.random.key(seed), 7)
    return {
        "density": jnp.clip(2.0 * jax.random.uniform(splits[0], (STATES, NX, NY, NZ), jnp.float32) ** shard_levels(splits[0], (STATES, NX, NY, NZ), ((0, 16), (1, 32)), -0.2, 0.2), 0.0, 2.0),
        "levels": jnp.clip(jax.random.uniform(splits[1], (LEVELS,), jnp.float32, 0.1, 0.9), 0.1, 0.9),
        "rate_index": touch_ends(jax.random.randint(splits[2], (STATES, 3), 0, LEVELS), jax.random.fold_in(splits[2], 1), 0, LEVELS - 1).astype(jnp.int32),
        "on_rate": jnp.clip(jnp.exp(jax.random.uniform(splits[3], (STATE_BITS,), jnp.float32, math.log(0.2), math.log(3.0))), 0.2, 3.0),
        "off_rate": jnp.clip(jnp.exp(jax.random.uniform(splits[4], (STATE_BITS,), jnp.float32, math.log(0.2), math.log(3.0))), 0.2, 3.0),
        "gene_order": jax.random.permutation(splits[5], BLOCKS).astype(jnp.int32),
    }


DIFF = 1.0
TIME_STEP = 0.15


def along(field, drift, axis):
    pads = [(0, 0)] * 4
    pads[axis] = (1, 1)
    padded = jnp.pad(field, pads)
    dpad = jnp.pad(drift, pads)
    size = field.shape[axis]
    upper = lax.slice_in_dim(padded, 2, size + 2, axis=axis)
    lower = lax.slice_in_dim(padded, 0, size, axis=axis)
    d_up = lax.slice_in_dim(dpad, 2, size + 2, axis=axis)
    d_low = lax.slice_in_dim(dpad, 0, size, axis=axis)
    return DIFF * (upper - 2.0 * field + lower) - 0.5 * (d_up * upper - d_low * lower)


def diffuse_group(pair):
    group_field, group_level = pair
    coord_x = (jnp.arange(NX, dtype=jnp.float32) + 0.5) / NX
    coord_y = (jnp.arange(NY, dtype=jnp.float32) + 0.5) / NY
    coord_z = (jnp.arange(NZ, dtype=jnp.float32) + 0.5) / NZ
    drift_x = (group_level[:, 0, None] - coord_x[None, :])[:, :, None, None]
    drift_y = (group_level[:, 1, None] - coord_y[None, :])[:, None, :, None]
    drift_z = (group_level[:, 2, None] - coord_z[None, :])[:, None, None, :]

    def one_step(step, field):
        change = along(field, drift_x, 1) + along(field, drift_y, 2) + along(field, drift_z, 3)
        return field + TIME_STEP * change

    return lax.fori_loop(0, SUBSTEPS, one_step, group_field)


def reference(density, levels, rate_index, on_rate, off_rate, gene_order):
    states = density.shape[0]
    groups = 16
    level_of = levels[rate_index]
    coord_x = (jnp.arange(NX, dtype=jnp.float32) + 0.5) / NX
    state_ids = jnp.arange(states, dtype=jnp.int32)
    hill = 0.1 + coord_x ** 2 / (0.09 + coord_x ** 2)
    grouped_level = level_of.reshape((groups, states // groups, 3))
    field = density
    for block in range(BLOCKS):
        grouped = field.reshape((groups, states // groups) + field.shape[1:])
        field = lax.map(diffuse_group, (grouped, grouped_level)).reshape(field.shape)
        bit = (STATE_BITS - 1 - gene_order[block]).astype(jnp.int32)
        mate_ids = jnp.bitwise_xor(state_ids, jnp.left_shift(jnp.int32(1), bit))
        mate = field[mate_ids]
        high = (jnp.bitwise_and(jnp.right_shift(state_ids, bit), 1) == 1)[:, None, None, None]
        act = (on_rate[bit] * hill)[None, :, None, None]
        rate = act + off_rate[bit]
        share = act / rate
        decay = jnp.exp(-rate)
        low_part = jnp.where(high, mate, field)
        high_part = jnp.where(high, field, mate)
        total = low_part + high_part
        new_high = share * total + (high_part - share * total) * decay
        field = jnp.where(high, new_high, total - new_high)
    return field
```

```python
from functools import partial

import jax
import jax.numpy as jnp
from jax import lax
from jax.experimental import pallas as pl
from jax.experimental.pallas import tpu as pltpu
from jax.sharding import PartitionSpec as P

STATE_BITS = 8
BLOCKS = 4
SUBSTEPS = 6
DIFF = 1.0
TIME_STEP = 0.15
SIDE = TIME_STEP * DIFF
HALF = 0.5 * TIME_STEP
CENTRE = 1.0 - 6.0 * TIME_STEP * DIFF


def split_rows(ref, state, layer):
    even = ref[state, layer, pl.ds(0, 8, stride=2), :]
    odd = ref[state, layer, pl.ds(1, 8, stride=2), :]
    return even, odd


def evolve_state(state, own, near, far, lev, ux, vx, core, first_x, total_x, width, store):
    size_y, size_z = own.shape[2], own.shape[3]
    shape = (8, size_z)
    lx = jnp.broadcast_to(lev[state, 0:1, :], shape)
    ly = jnp.broadcast_to(lev[state, 1:2, :], shape)
    lz = jnp.broadcast_to(lev[state, 2:3, :], shape)
    span = width + 2 * SUBSTEPS
    for c in range(1, span - 1):
        cell = first_x - SUBSTEPS + c
        inside = jnp.where((cell >= 0) & (cell < total_x), 1.0, 0.0)
        above = (cell.astype(jnp.float32) + 1.5) / total_x
        below = (cell.astype(jnp.float32) - 0.5) / total_x
        ux[c] = (SIDE - HALF * (lx - above)) * inside
        vx[c] = (SIDE + HALF * (lx - below)) * inside
    row = lax.broadcasted_iota(jnp.int32, shape, 0)
    col = lax.broadcasted_iota(jnp.int32, shape, 1)
    y_even = (2 * row).astype(jnp.float32)
    zc = col.astype(jnp.float32)
    ue = SIDE - HALF * (ly - (y_even + 1.5) / size_y)
    ve = jnp.where(row == 0, 0.0, SIDE + HALF * (ly - (y_even - 0.5) / size_y))
    uo = jnp.where(row == 7, 0.0, SIDE - HALF * (ly - (y_even + 2.5) / size_y))
    vo = SIDE + HALF * (ly - (y_even + 0.5) / size_y)
    uz = jnp.where(col == size_z - 1, 0.0, SIDE - HALF * (lz - (zc + 1.5) / size_z))
    vz = jnp.where(col == 0, 0.0, SIDE + HALF * (lz - (zc - 0.5) / size_z))

    is_low = core == 0
    field = []
    for c in range(width):
        a, b = split_rows(near, state, c), split_rows(far, state, c)
        field.append(tuple(jnp.where(is_low, q, p) for p, q in zip(a, b)))
    for c in range(width):
        field.append(split_rows(own, state, c))
    for c in range(width):
        a, b = split_rows(near, state, c), split_rows(far, state, c)
        field.append(tuple(jnp.where(is_low, p, q) for p, q in zip(a, b)))

    for step in range(SUBSTEPS):
        fresh = []
        base = step + 1
        for i in range(1, len(field) - 1):
            c = base + i - 1
            even, odd = field[i]
            u, v = ux[c], vx[c]
            new = []
            for k, mid in enumerate((even, odd)):
                up, down = field[i + 1][k], field[i - 1][k]
                if k == 0:
                    y_part = ue * odd + ve * pltpu.roll(odd, 1, 0)
                else:
                    y_part = uo * pltpu.roll(even, 7, 0) + vo * even
                z_part = uz * pltpu.roll(mid, size_z - 1, 1) + vz * pltpu.roll(mid, 1, 1)
                x_part = u * up + v * down
                new.append((CENTRE * mid + x_part) + (y_part + z_part))
            fresh.append(tuple(new))
        field = fresh
    for c in range(width):
        store(c, field[c][0], field[c][1])


def switch_factors(first_x, layer, total_x, on, off, shape):
    u = (jnp.full(shape, first_x + layer, jnp.int32).astype(jnp.float32) + 0.5) / total_x
    act = on * (0.1 + u * u / (0.09 + u * u))
    rate = act + off
    return act / rate, jnp.exp(-rate)


def block_kernel(block, order, on_rate, off_rate, own, near, far, lev, out, ux, vx):
    count, width, size_y, size_z = own.shape
    place = lax.axis_index("prot")
    total_x = width * lax.axis_size("prot")
    first_x = place * width
    core = lax.rem(place, 2)

    def one(state, carry):
        def store(c, even, odd):
            out[state, c, pl.ds(0, 8, stride=2), :] = even
            out[state, c, pl.ds(1, 8, stride=2), :] = odd

        evolve_state(state, own, near, far, lev, ux, vx, core, first_x, total_x, width, store)
        return carry

    lax.fori_loop(0, count, one, 0)

    gene = order[block]
    on, off = on_rate[STATE_BITS - 1 - gene], off_rate[STATE_BITS - 1 - gene]
    bit = count.bit_length() - 2 - gene
    stride = jnp.left_shift(1, bit)
    for c in range(width):
        share, decay = switch_factors(first_x, c, total_x, on, off, (size_y, size_z))

        def pair(k, carry, c=c, share=share, decay=decay):
            low = jnp.bitwise_and(k, stride - 1)
            s = 2 * (k - low) + low
            t = s + stride
            qs, qt = out[s, c], out[t, c]
            total = qs + qt
            part = share * total
            high = part + (qt - part) * decay
            out[t, c] = high
            out[s, c] = total - high
            return carry

        lax.fori_loop(0, count // 2, pair, 0, unroll=True)


def run_block(block, order, on_rate, off_rate, own, near, far, lev):
    smem = pl.BlockSpec(memory_space=pltpu.SMEM)
    vmem = pl.BlockSpec(memory_space=pltpu.VMEM)
    span = own.shape[1] + 2 * SUBSTEPS
    updates = own.size * 11
    return pl.pallas_call(
        partial(block_kernel, block),
        out_shape=jax.ShapeDtypeStruct(own.shape, jnp.float32),
        in_specs=[smem] * 3 + [vmem] * 4,
        out_specs=vmem,
        scratch_shapes=[pltpu.VMEM((span, 8, own.shape[3]), jnp.float32)] * 2,
        compiler_params=pltpu.CompilerParams(vmem_limit_bytes=32 * 1024 * 1024),
        cost_estimate=pl.CostEstimate(flops=updates * 14, bytes_accessed=own.size * 16, transcendentals=0),
        name=f"block{block}",
    )(order, on_rate, off_rate, own, near, far, lev)


def local(density, levels, rate_index, on_rate, off_rate, gene_order):
    count, width, size_y, size_z = density.shape
    size = lax.axis_size("prot")
    onehot = rate_index[:, :, None] == jnp.arange(levels.shape[0], dtype=jnp.int32)[None, None, :]
    level_of = jnp.sum(jnp.where(onehot, levels[None, None, :], 0.0), axis=-1)
    rows = jnp.concatenate([level_of, jnp.zeros((count, 5), jnp.float32)], axis=1)
    rows = jnp.broadcast_to(rows[:, :, None], (count, 8, size_z))
    both = jnp.concatenate([density.reshape(count, width * size_y, size_z), rows], axis=1)
    both = lax.all_to_all(both, "gene", 0, 0, tiled=True)
    field = both[:, : width * size_y].reshape(density.shape)
    lev = both[:, width * size_y :]
    inner = [(i, i ^ 1) for i in range(size)]
    outer = [(i, i + 1) for i in range(1, size - 1, 2)] + [(i + 1, i) for i in range(1, size - 1, 2)]
    for block in range(BLOCKS):
        far = lax.ppermute(field, "prot", outer)
        near = lax.ppermute(field, "prot", inner)
        field = run_block(block, gene_order, on_rate, off_rate, field, near, far, lev)
    return lax.all_to_all(field, "gene", 0, 0, tiled=True)


def solution(mesh):
    in_specs = (P("gene", "prot", None, None), P(), P("gene", None), P(), P(), P())
    out_specs = P("gene", "prot", None, None)
    return jax.shard_map(local, mesh=mesh, in_specs=in_specs, out_specs=out_specs, check_vma=False)
```

```python
from functools import partial

import jax
import jax.numpy as jnp
from jax import lax
from jax.experimental import pallas as pl
from jax.experimental.pallas import tpu as pltpu
from jax.sharding import PartitionSpec as P

STATE_BITS = 8
BLOCKS = 4
SUBSTEPS = 6
DIFF = 1.0
TIME_STEP = 0.15
SIDE = TIME_STEP * DIFF
HALF = 0.5 * TIME_STEP
ROWS = 8
CENTRE = 1.0 - 6.0 * TIME_STEP * DIFF


def switch_factors(first_x, layer, total_x, on, off, shape):
    u = (jnp.full(shape, first_x + layer, jnp.int32).astype(jnp.float32) + 0.5) / total_x
    act = on * (0.1 + u * u / (0.09 + u * u))
    rate = act + off
    return act / rate, jnp.exp(-rate)


def spread(place, bit, value):
    low = jnp.bitwise_and(place, jnp.left_shift(1, bit) - 1)
    return 2 * (place - low) + low + jnp.left_shift(value, bit)


def swap_bits(value):
    row = lax.broadcasted_iota(jnp.int32, value.shape, 0)
    col = lax.broadcasted_iota(jnp.int32, value.shape, 1)
    lanes = value.shape[1]
    for k in (1, 2, 4):
        row_set, col_set = jnp.bitwise_and(row, k) != 0, jnp.bitwise_and(col, k) != 0
        down = pltpu.roll(pltpu.roll(value, k, 0), lanes - k, 1)
        up = pltpu.roll(pltpu.roll(value, ROWS - k, 0), k, 1)
        value = jnp.where(row_set == col_set, value, jnp.where(row_set, down, up))
    return value


def entry_kernel(width, size_y, order, on_rate, off_rate, both, low, high, x_table, y_table, z_table, mix_table, packed, turned):
    last_bit = BLOCKS - 1 - order[BLOCKS - 1]
    layer_rows = width * size_y
    size_z = both.shape[2]
    count = both.shape[0] // 2
    shape = (ROWS, size_z)
    place = lax.axis_index("prot")
    total_x = width * lax.axis_size("prot")
    first_x = place * width
    row = lax.broadcasted_iota(jnp.int32, shape, 0)
    col = lax.broadcasted_iota(jnp.int32, shape, 1)
    lane_state = jnp.bitwise_and(lax.broadcasted_iota(jnp.int32, (1, size_z), 1), count - 1)
    for chunk in range(2):
        for k in range(count):
            packed[chunk, pl.ds(k * layer_rows, layer_rows), :] = both[spread(k, last_bit, chunk), 0:layer_rows, :]

    def layer(x, carry):
        for chunk in range(2):
            for y in range(size_y):
                turned[chunk, pl.ds(y * ROWS, ROWS), :] = swap_bits(
                    packed[chunk, pl.ds(x * size_y + y, count, stride=layer_rows), :]
                )
        for chunk, out in enumerate((low, high)):
            for q in range(2 * ROWS):
                out[x, q] = turned[chunk, pl.ds((q % 2) * ROWS + q // 2, ROWS, stride=2 * ROWS), :]
        return carry

    lax.fori_loop(0, width, layer, 0)
    for chunk in range(2):
        lines = []
        for r in range(3):
            line = jnp.zeros((1, size_z), jnp.float32)
            for k in range(count):
                line = jnp.where(lane_state == k, both[spread(k, last_bit, chunk), layer_rows + r : layer_rows + r + 1, :], line)
            lines.append(jnp.broadcast_to(line, shape))
        lx, ly, lz = lines
        for c in range(x_table.shape[2]):
            cell = first_x - SUBSTEPS + c
            inside = jnp.where((cell >= 0) & (cell < total_x), 1.0, 0.0)
            centre = jnp.full(shape, cell, jnp.int32).astype(jnp.float32)
            x_table[chunk, 0, c] = (SIDE - HALF * (lx - (centre + 1.5) / total_x)) * inside
            x_table[chunk, 1, c] = (SIDE + HALF * (lx - (centre - 0.5) / total_x)) * inside
        y_even = (2 * row).astype(jnp.float32)
        y_table[chunk, 0] = SIDE - HALF * (ly - (y_even + 1.5) / size_y)
        y_table[chunk, 1] = jnp.where(row == 0, 0.0, SIDE + HALF * (ly - (y_even - 0.5) / size_y))
        y_table[chunk, 2] = jnp.where(row == ROWS - 1, 0.0, SIDE - HALF * (ly - (y_even + 2.5) / size_y))
        y_table[chunk, 3] = SIDE + HALF * (ly - (y_even + 0.5) / size_y)
        for j in range(ROWS):
            z = jnp.bitwise_and(col, -ROWS) + j
            zc = z.astype(jnp.float32)
            z_table[chunk, 0, j] = jnp.where(z == size_z - 1, 0.0, SIDE - HALF * (lz - (zc + 1.5) / size_z))
            z_table[chunk, 1, j] = jnp.where(z == 0, 0.0, SIDE + HALF * (lz - (zc - 0.5) / size_z))
    for block in range(BLOCKS):
        bit = STATE_BITS - 1 - order[block]
        for c in range(width):
            share, decay = switch_factors(first_x, c, total_x, on_rate[bit], off_rate[bit], shape)
            mix_table[block, 0, c] = share
            mix_table[block, 1, c] = decay


def enter(scalars, both, width, size_y):
    lanes = both.shape[2]
    smem = pl.BlockSpec(memory_space=pltpu.SMEM)
    vmem = pl.BlockSpec(memory_space=pltpu.VMEM)
    tile = (ROWS, lanes)
    chunk = (width, 2 * ROWS) + tile
    dims = [chunk, chunk, (2, 2, width + 2 * SUBSTEPS) + tile, (2, 4) + tile, (2, 2, ROWS) + tile, (BLOCKS, 2, width) + tile]
    return pl.pallas_call(
        partial(entry_kernel, width, size_y),
        out_shape=tuple(jax.ShapeDtypeStruct(d, jnp.float32) for d in dims),
        in_specs=[smem] * 3 + [vmem],
        out_specs=(vmem,) * len(dims),
        scratch_shapes=[
            pltpu.VMEM((2, ROWS * width * size_y, lanes), jnp.float32),
            pltpu.VMEM((2, size_y * ROWS, lanes), jnp.float32),
        ],
        compiler_params=pltpu.CompilerParams(vmem_limit_bytes=32 * 1024 * 1024),
        name="enter",
    )(*scalars, both)


def block_kernel(mode, block, chunk, order, own, left, right, x_table, y_table, z_table, mix_table, *rest):
    rest = list(rest)
    other = rest.pop(0) if mode == "join" else None
    out, first, second = rest[:3]
    width, parts, rows, lanes = own.shape
    size_y, count = 2 * rows, ROWS
    shape = (rows, lanes)
    span = width + 2 * SUBSTEPS
    last_bit = BLOCKS - 1 - order[BLOCKS - 1]
    bit = BLOCKS - 1 - order[block]
    inner_bit = jnp.where(bit > last_bit, bit - 1, bit)
    ue, ve, uo, vo = (y_table[chunk, k] for k in range(4))
    col = lax.broadcasted_iota(jnp.int32, shape, 1)
    is_high = jnp.bitwise_and(jnp.right_shift(col, inner_bit), 1) == 1
    apart = jnp.left_shift(1, inner_bit)

    def finish(c, q, value):
        if mode != "inside":
            return value
        mate = jnp.where(is_high, pltpu.roll(value, apart, 1), pltpu.roll(value, lanes - apart, 1))
        total = value + mate
        part = mix_table[block, 0, c] * total
        up = part + (jnp.where(is_high, value, mate) - part) * mix_table[block, 1, c]
        return jnp.where(is_high, up, total - up)

    def given(c, q):
        return (left, own, right)[c // width][c % width, q]

    read = given
    for step in range(SUBSTEPS):
        target = (first, second)[step % 2]
        final = step == SUBSTEPS - 1
        for c in range(step + 1, span - 1 - step):
            u, v = x_table[chunk, 0, c], x_table[chunk, 1, c]
            mids = [read(c, q) for q in range(parts)]
            sums = [CENTRE * mids[q] + (u * read(c + 1, q) + v * read(c - 1, q)) for q in range(parts)]
            fresh = []
            for q in range(parts):
                j, odd = q // 2, q % 2
                pair = mids[q ^ 1]
                if odd:
                    y_part = uo * pltpu.roll(pair, rows - 1, 0) + vo * pair
                else:
                    y_part = ue * pair + ve * pltpu.roll(pair, 1, 0)
                z_up = mids[q + 2] if q + 2 < parts else pltpu.roll(mids[odd], lanes - ROWS, 1)
                z_down = mids[q - 2] if q >= 2 else pltpu.roll(mids[parts - 2 + odd], ROWS, 1)
                z_part = z_table[chunk, 0, j] * z_up + z_table[chunk, 1, j] * z_down
                fresh.append(sums[q] + (y_part + z_part))
            for q in range(parts):
                if final and mode != "join":
                    out[c - width, q] = finish(c - width, q, fresh[q])
                else:
                    target[c, q] = fresh[q]
        read = lambda c, q, ref=target: ref[c, q]
    if mode != "join":
        return
    source = target
    packed, turned = rest[3:]
    layer_rows = width * size_y

    def leave(c, carry):
        share, decay = mix_table[block, 0, c], mix_table[block, 1, c]
        for q in range(parts):
            low, high = other[c, q], source[width + c, q]
            total = low + high
            part = share * total
            up = part + (high - part) * decay
            at = pl.ds((q % 2) * ROWS + q // 2, ROWS, stride=2 * ROWS)
            turned[0, at, :] = total - up
            turned[1, at, :] = up
        for y in range(size_y):
            for half in range(2):
                packed[half, pl.ds(c * size_y + y, count, stride=layer_rows), :] = swap_bits(
                    turned[half, pl.ds(y * ROWS, ROWS), :]
                )
        return carry

    lax.fori_loop(0, width, leave, 0)
    for half in range(2):
        for k in range(count):
            out[spread(k, last_bit, half)] = packed[half, pl.ds(k * layer_rows, layer_rows), :]


def run_block(mode, block, chunk, order, own, left, right, tables, other=None):
    smem = pl.BlockSpec(memory_space=pltpu.SMEM)
    vmem = pl.BlockSpec(memory_space=pltpu.VMEM)
    width, parts, rows, lanes = own.shape
    span = width + 2 * SUBSTEPS
    layer_rows = width * 2 * rows
    out = jax.ShapeDtypeStruct(own.shape, jnp.float32)
    scratch = [(span, parts, rows, lanes)] * 2
    if mode == "join":
        out = jax.ShapeDtypeStruct((2 * ROWS, layer_rows, lanes), jnp.float32)
        scratch = scratch + [(2, ROWS * layer_rows, lanes), (2, ROWS * 2 * rows, lanes)]
    extra = () if other is None else (other,)
    updates = own.size * 11
    return pl.pallas_call(
        partial(block_kernel, mode, block, chunk),
        out_shape=out,
        in_specs=[smem] + [vmem] * (3 + len(tables) + len(extra)),
        out_specs=vmem,
        scratch_shapes=[pltpu.VMEM(dims, jnp.float32) for dims in scratch],
        compiler_params=pltpu.CompilerParams(vmem_limit_bytes=32 * 1024 * 1024),
        cost_estimate=pl.CostEstimate(flops=updates * 14, bytes_accessed=own.size * 16, transcendentals=0),
        name=f"block{block}_{chunk}",
    )(order, own, left, right, *tables, *extra)


def local(density, levels, rate_index, on_rate, off_rate, gene_order):
    count, width, size_y, size_z = density.shape
    size = lax.axis_size("prot")
    onehot = rate_index[:, :, None] == jnp.arange(levels.shape[0], dtype=jnp.int32)[None, None, :]
    level_of = jnp.sum(jnp.where(onehot, levels[None, None, :], 0.0), axis=-1)
    rows = jnp.concatenate([level_of, jnp.zeros((count, ROWS - 3), jnp.float32)], axis=1)
    rows = jnp.broadcast_to(rows[:, :, None], (count, ROWS, size_z))
    both = jnp.concatenate([density.reshape(count, width * size_y, size_z), rows], axis=1)
    both = lax.all_to_all(both, "gene", 0, 0, tiled=True)
    low, high, *tables = enter((gene_order, on_rate, off_rate), both, width, size_y)
    parts = [low, high]
    forward = [(i, i + 1) for i in range(size - 1)]
    backward = [(i + 1, i) for i in range(size - 1)]
    for block in range(BLOCKS):
        sides = [(lax.ppermute(p, "prot", forward), lax.ppermute(p, "prot", backward)) for p in parts]
        if block < BLOCKS - 1:
            parts = [run_block("inside", block, c, gene_order, parts[c], *sides[c], tables) for c in range(2)]
        else:
            done = run_block("plain", block, 0, gene_order, parts[0], *sides[0], tables)
            done = run_block("join", block, 1, gene_order, parts[1], *sides[1], tables, done)
    done = lax.all_to_all(done, "gene", 0, 0, tiled=True)
    return done.reshape(density.shape)


def solution(mesh):
    in_specs = (P("gene", "prot", None, None), P(), P("gene", None), P(), P(), P())
    out_specs = P("gene", "prot", None, None)
    return jax.shard_map(local, mesh=mesh, in_specs=in_specs, out_specs=out_specs, check_vma=False)
```

```python
from functools import partial

import jax
import jax.numpy as jnp
from jax import lax
from jax.experimental import pallas as pl
from jax.experimental.pallas import tpu as pltpu
from jax.sharding import PartitionSpec as P

STATE_BITS = 8
BLOCKS = 4
SUBSTEPS = 6
DIFF = 1.0
TIME_STEP = 0.15
SIDE = TIME_STEP * DIFF
HALF = 0.5 * TIME_STEP
ROWS = 8
CENTRE = 1.0 - 6.0 * TIME_STEP * DIFF


def switch_factors(first_x, layer, total_x, on, off, shape):
    u = (jnp.full(shape, first_x + layer, jnp.int32).astype(jnp.float32) + 0.5) / total_x
    act = on * (0.1 + u * u / (0.09 + u * u))
    rate = act + off
    return act / rate, jnp.exp(-rate)


def spread(place, bit, value):
    low = jnp.bitwise_and(place, jnp.left_shift(1, bit) - 1)
    return 2 * (place - low) + low + jnp.left_shift(value, bit)


def swap_bits(value):
    row = lax.broadcasted_iota(jnp.int32, value.shape, 0)
    col = lax.broadcasted_iota(jnp.int32, value.shape, 1)
    lanes = value.shape[1]
    for k in (1, 2, 4):
        row_set, col_set = jnp.bitwise_and(row, k) != 0, jnp.bitwise_and(col, k) != 0
        down = pltpu.roll(pltpu.roll(value, k, 0), lanes - k, 1)
        up = pltpu.roll(pltpu.roll(value, ROWS - k, 0), k, 1)
        value = jnp.where(row_set == col_set, value, jnp.where(row_set, down, up))
    return value


def entry_kernel(chunk, layer_rows, order, both, out, packed, turned):
    last_bit = BLOCKS - 1 - order[BLOCKS - 1]
    size_y = turned.shape[0] // ROWS
    count = both.shape[0] // 2
    for k in range(count):
        packed[pl.ds(k * layer_rows, layer_rows), :] = both[spread(k, last_bit, chunk), 0:layer_rows, :]

    def layer(x, carry):
        for y in range(size_y):
            turned[pl.ds(y * ROWS, ROWS), :] = swap_bits(packed[pl.ds(x * size_y + y, count, stride=layer_rows), :])
        for q in range(2 * ROWS):
            out[x, q] = turned[pl.ds((q % 2) * ROWS + q // 2, ROWS, stride=2 * ROWS), :]
        return carry

    lax.fori_loop(0, layer_rows // size_y, layer, 0)


def enter(chunk, order, both, width, size_y):
    lanes = both.shape[2]
    vmem = pl.BlockSpec(memory_space=pltpu.VMEM)
    return pl.pallas_call(
        partial(entry_kernel, chunk, width * size_y),
        out_shape=jax.ShapeDtypeStruct((width, 2 * ROWS, ROWS, lanes), jnp.float32),
        in_specs=[pl.BlockSpec(memory_space=pltpu.SMEM), vmem],
        out_specs=vmem,
        scratch_shapes=[
            pltpu.VMEM((ROWS * width * size_y, lanes), jnp.float32),
            pltpu.VMEM((size_y * ROWS, lanes), jnp.float32),
        ],
        compiler_params=pltpu.CompilerParams(vmem_limit_bytes=32 * 1024 * 1024),
        name=f"enter{chunk}",
    )(order, both)


def tables_kernel(width, size_y, order, on_rate, off_rate, levels, both, x_table, y_table, z_table, mix_table):
    last_bit = BLOCKS - 1 - order[BLOCKS - 1]
    size_z = both.shape[2]
    count = both.shape[0] // 2
    layer_rows = width * size_y
    shape = (ROWS, size_z)
    place = lax.axis_index("prot")
    total_x = width * lax.axis_size("prot")
    first_x = place * width
    row = lax.broadcasted_iota(jnp.int32, shape, 0)
    col = lax.broadcasted_iota(jnp.int32, shape, 1)
    lane_state = jnp.bitwise_and(lax.broadcasted_iota(jnp.int32, (1, size_z), 1), count - 1)
    for chunk in range(2):
        lines = []
        for r in range(3):
            line = jnp.zeros((1, size_z), jnp.float32)
            for k in range(count):
                line = jnp.where(lane_state == k, both[spread(k, last_bit, chunk), layer_rows + r : layer_rows + r + 1, :], line)
            level = jnp.zeros((1, size_z), jnp.float32)
            for m in range(levels.shape[0]):
                level = jnp.where(line == float(m), levels[m], level)
            lines.append(jnp.broadcast_to(level, shape))
        lx, ly, lz = lines
        for c in range(x_table.shape[2]):
            cell = first_x - SUBSTEPS + c
            inside = jnp.where((cell >= 0) & (cell < total_x), 1.0, 0.0)
            centre = jnp.full(shape, cell, jnp.int32).astype(jnp.float32)
            x_table[chunk, 0, c] = (SIDE - HALF * (lx - (centre + 1.5) / total_x)) * inside
            x_table[chunk, 1, c] = (SIDE + HALF * (lx - (centre - 0.5) / total_x)) * inside
        y_even = (2 * row).astype(jnp.float32)
        y_table[chunk, 0] = SIDE - HALF * (ly - (y_even + 1.5) / size_y)
        y_table[chunk, 1] = jnp.where(row == 0, 0.0, SIDE + HALF * (ly - (y_even - 0.5) / size_y))
        y_table[chunk, 2] = jnp.where(row == ROWS - 1, 0.0, SIDE - HALF * (ly - (y_even + 2.5) / size_y))
        y_table[chunk, 3] = SIDE + HALF * (ly - (y_even + 0.5) / size_y)
        for j in range(ROWS):
            z = jnp.bitwise_and(col, -ROWS) + j
            zc = z.astype(jnp.float32)
            z_table[chunk, 0, j] = jnp.where(z == size_z - 1, 0.0, SIDE - HALF * (lz - (zc + 1.5) / size_z))
            z_table[chunk, 1, j] = jnp.where(z == 0, 0.0, SIDE + HALF * (lz - (zc - 0.5) / size_z))
    for block in range(BLOCKS):
        bit = STATE_BITS - 1 - order[block]
        for c in range(width):
            share, decay = switch_factors(first_x, c, total_x, on_rate[bit], off_rate[bit], shape)
            mix_table[block, 0, c] = share
            mix_table[block, 1, c] = decay


def make_tables(scalars, both, width, size_y):
    smem = pl.BlockSpec(memory_space=pltpu.SMEM)
    vmem = pl.BlockSpec(memory_space=pltpu.VMEM)
    tile = (ROWS, both.shape[2])
    dims = [(2, 2, width + 2 * SUBSTEPS) + tile, (2, 4) + tile, (2, 2, ROWS) + tile, (BLOCKS, 2, width) + tile]
    return pl.pallas_call(
        partial(tables_kernel, width, size_y),
        out_shape=tuple(jax.ShapeDtypeStruct(d, jnp.float32) for d in dims),
        in_specs=[smem] * len(scalars) + [vmem],
        out_specs=(vmem,) * len(dims),
        compiler_params=pltpu.CompilerParams(vmem_limit_bytes=32 * 1024 * 1024),
        name="tables",
    )(*scalars, both)


def block_kernel(mode, block, chunk, order, own, left, right, x_table, y_table, z_table, mix_table, *rest):
    rest = list(rest)
    other = rest.pop(0) if mode == "join" else None
    out, first, second = rest[:3]
    width, parts, rows, lanes = own.shape
    size_y, count = 2 * rows, ROWS
    shape = (rows, lanes)
    span = width + 2 * SUBSTEPS
    last_bit = BLOCKS - 1 - order[BLOCKS - 1]
    bit = BLOCKS - 1 - order[block]
    inner_bit = jnp.where(bit > last_bit, bit - 1, bit)
    ue, ve, uo, vo = (y_table[chunk, k] for k in range(4))
    col = lax.broadcasted_iota(jnp.int32, shape, 1)
    is_high = jnp.bitwise_and(jnp.right_shift(col, inner_bit), 1) == 1
    apart = jnp.left_shift(1, inner_bit)

    def finish(c, q, value):
        mate = jnp.where(is_high, pltpu.roll(value, apart, 1), pltpu.roll(value, lanes - apart, 1))
        total = value + mate
        part = mix_table[block, 0, c] * total
        up = part + (jnp.where(is_high, value, mate) - part) * mix_table[block, 1, c]
        return jnp.where(is_high, up, total - up)

    def given(c, q):
        return (left, own, right)[c // width][c % width, q]

    read = given
    for step in range(SUBSTEPS):
        target = (first, second)[step % 2]
        final = step == SUBSTEPS - 1
        for c in range(step + 1, span - 1 - step):
            u, v = x_table[chunk, 0, c], x_table[chunk, 1, c]
            mids = [read(c, q) for q in range(parts)]
            sums = [CENTRE * mids[q] + (u * read(c + 1, q) + v * read(c - 1, q)) for q in range(parts)]
            fresh = []
            for q in range(parts):
                j, odd = q // 2, q % 2
                pair = mids[q ^ 1]
                if odd:
                    y_part = uo * pltpu.roll(pair, rows - 1, 0) + vo * pair
                else:
                    y_part = ue * pair + ve * pltpu.roll(pair, 1, 0)
                z_up = mids[q + 2] if q + 2 < parts else pltpu.roll(mids[odd], lanes - ROWS, 1)
                z_down = mids[q - 2] if q >= 2 else pltpu.roll(mids[parts - 2 + odd], ROWS, 1)
                z_part = z_table[chunk, 0, j] * z_up + z_table[chunk, 1, j] * z_down
                fresh.append(sums[q] + (y_part + z_part))
            for q in range(parts):
                if final and mode == "inside":
                    out[c - width, q] = finish(c - width, q, fresh[q])
                else:
                    target[c, q] = fresh[q]
        read = lambda c, q, ref=target: ref[c, q]
    if mode == "inside":
        return
    source = target
    packed, turned = (out, rest[3]) if mode == "plain" else rest[3:]
    layer_rows = width * size_y

    def leave(c, carry):
        for q in range(parts):
            turned[pl.ds((q % 2) * ROWS + q // 2, ROWS, stride=2 * ROWS), :] = source[width + c, q]
        for y in range(size_y):
            packed[pl.ds(c * size_y + y, count, stride=layer_rows), :] = swap_bits(turned[pl.ds(y * ROWS, ROWS), :])
        return carry

    lax.fori_loop(0, width, leave, 0)
    if mode == "plain":
        return
    for c in range(width):
        share, decay = mix_table[block, 0, c], mix_table[block, 1, c]
        for k in range(count):
            for r in range(c * size_y, (c + 1) * size_y, ROWS):
                low, high = other[pl.ds(k * layer_rows + r, ROWS), :], packed[pl.ds(k * layer_rows + r, ROWS), :]
                total = low + high
                part = share * total
                up = part + (high - part) * decay
                out[spread(k, last_bit, 1), pl.ds(r, ROWS), :] = up
                out[spread(k, last_bit, 0), pl.ds(r, ROWS), :] = total - up


def run_block(mode, block, chunk, order, own, left, right, tables, other=None):
    smem = pl.BlockSpec(memory_space=pltpu.SMEM)
    vmem = pl.BlockSpec(memory_space=pltpu.VMEM)
    width, parts, rows, lanes = own.shape
    span = width + 2 * SUBSTEPS
    layer_rows = width * 2 * rows
    out = jax.ShapeDtypeStruct(own.shape, jnp.float32)
    scratch = [(span, parts, rows, lanes)] * 2
    if mode == "plain":
        out = jax.ShapeDtypeStruct((ROWS * layer_rows, lanes), jnp.float32)
        scratch = scratch + [(ROWS * 2 * rows, lanes)]
    if mode == "join":
        out = jax.ShapeDtypeStruct((2 * ROWS, layer_rows, lanes), jnp.float32)
        scratch = scratch + [(ROWS * layer_rows, lanes), (ROWS * 2 * rows, lanes)]
    extra = () if other is None else (other,)
    updates = own.size * 11
    return pl.pallas_call(
        partial(block_kernel, mode, block, chunk),
        out_shape=out,
        in_specs=[smem] + [vmem] * (3 + len(tables) + len(extra)),
        out_specs=vmem,
        scratch_shapes=[pltpu.VMEM(dims, jnp.float32) for dims in scratch],
        compiler_params=pltpu.CompilerParams(vmem_limit_bytes=32 * 1024 * 1024),
        cost_estimate=pl.CostEstimate(flops=updates * 14, bytes_accessed=own.size * 16, transcendentals=0),
        name=f"block{block}_{chunk}",
    )(order, own, left, right, *tables, *extra)


def local(density, levels, rate_index, on_rate, off_rate, gene_order):
    count, width, size_y, size_z = density.shape
    size = lax.axis_size("prot")
    rows = jnp.pad(rate_index.astype(jnp.float32), ((0, 0), (0, ROWS - rate_index.shape[1])))
    rows = jnp.broadcast_to(rows[:, :, None], (count, ROWS, size_z))
    both = jnp.concatenate([density.reshape(count, width * size_y, size_z), rows], axis=1)
    both = lax.all_to_all(both, "gene", 0, 0, tiled=True)
    parts = [enter(chunk, gene_order, both, width, size_y) for chunk in range(2)]
    levels, parts[1] = lax.optimization_barrier((levels, parts[1]))
    tables = make_tables((gene_order, on_rate, off_rate, levels), both, width, size_y)
    forward = [(i, i + 1) for i in range(size - 1)]
    backward = [(i + 1, i) for i in range(size - 1)]
    for block in range(BLOCKS):
        sides = [(lax.ppermute(p, "prot", forward), lax.ppermute(p, "prot", backward)) for p in parts]
        if block < BLOCKS - 1:
            parts = [run_block("inside", block, c, gene_order, parts[c], *sides[c], tables) for c in range(2)]
        else:
            done = run_block("plain", block, 0, gene_order, parts[0], *sides[0], tables)
            done = run_block("join", block, 1, gene_order, parts[1], *sides[1], tables, done)
    done = lax.all_to_all(done, "gene", 0, 0, tiled=True)
    return done.reshape(density.shape)


def solution(mesh):
    in_specs = (P("gene", "prot", None, None), P(), P("gene", None), P(), P(), P())
    out_specs = P("gene", "prot", None, None)
    return jax.shard_map(local, mesh=mesh, in_specs=in_specs, out_specs=out_specs, check_vma=False)
```
